32 devices in a mesh: group: 2 (over x), row: 16 (over z, y, core), col: 1.
Axes of the slice: x: 2, y: 2, z: 4, core: 2. Of those that a mesh axis runs over, the one named last changes fastest.
Arguments:
- pair: bfloat16 [256, 128, 128], P(('group', 'row'), 'col'), parts along dimension 0, may hold values from -6 to 6
- residue_mask: int32 [256], P('group'), parts along dimension 0, may hold values 0 or 1
- ln_gain: float32 [2, 128], replicated, may hold values from 0.1 to 1.9
- ln_bias: float32 [2, 128], replicated, may hold values from -0.45 to 0.45
- w_ab: bfloat16 [2, 128, 512], replicated, may hold values from -0.5 to 0.5
- w_gate: bfloat16 [2, 128, 128], replicated, may hold values from -0.5 to 0.5
- out_gain: float32 [2, 128], replicated, may hold values from 1.3 to 2.2
- out_bias: float32 [2, 128], replicated, may hold values from -1 to 1
- w_out: bfloat16 [2, 128, 128], replicated, may hold values from -0.110485435 to 0.110485435
Outputs:
- updated: bfloat16 [256, 128, 128], P(('group', 'row'), 'col'), parts along dimension 0
The draws below stay inside these ranges and needn't reach their ends.
There are 2 independent parts, one for each index of `group`. The reference program is written for one: setup_inputs(seed, part) draws one part's arguments, and reference() takes and returns one part's arrays. A program takes and returns all parts, laid end to end along the dimension named above; an argument that names none is the same for every part. Nothing has to cross between parts.
All inputs are finite; a program needn't handle non-finite values.
Results may differ from the reference program's by a relative error of at most 0.019.
Values may be sent and summed in bfloat16 or wider, within the bound.
A program may use at most 128 MiB of HBM per device.

```python
import jax
import jax.numpy as jnp
from jax import lax

C = 128
CH = 128
N = 128


def draw_pair(key, part):
    key = jax.random.fold_in(key, 11)
    base = jax.random.normal(key, (N, N, C), jnp.float32)
    return jnp.clip(base, -6.0, 6.0).astype(jnp.bfloat16)


def draw_ln_bias(key, part):
    key = jax.random.fold_in(key, 23)
    base = jax.random.normal(key, (2, C), jnp.float32)
    return 0.15 * jnp.clip(base, -3.0, 3.0)


def draw_out_gain(key, part):
    key = jax.random.fold_in(key, 37)
    base = jax.random.normal(key, (2, CH), jnp.float32)
    return 1.7 * jnp.exp(0.1 * jnp.clip(base, -2.5, 2.5))


def draw_w_out(key, part):
    key = jax.random.fold_in(key, 41)
    sign_key, size_key = jax.random.split(key)
    signs = jax.random.rademacher(sign_key, (2, CH, C), dtype=jnp.float32)
    sizes = jax.random.uniform(size_key, (2, CH, C), jnp.float32, 0.75, 1.25)
    return (signs * sizes * CH ** (-0.5)).astype(jnp.bfloat16)


def touch_ends(entries, key, least, high):
    shape = entries.shape
    index_at = [jax.random.randint(jax.random.fold_in(key, axis), (), 0, shape[axis]) for axis in range(len(shape))]
    entries = entries.at[tuple(index_at)].set(least)
    longest = shape.index(max(shape))
    index_at[longest] = (index_at[longest] + 1) % shape[longest]
    return entries.at[tuple(index_at)].set(high)


def gaussian(own_key, dims, spread, bound, held_as=jnp.bfloat16):
    return jnp.clip(spread * jax.random.normal(own_key, dims, jnp.float32), -bound, bound).astype(held_as)


def setup_inputs(seed: int = 0, part: int = 0) -> dict:
    keys = jax.random.split(jax.random.key(seed), 10)
    own_keys = jax.random.split(jax.random.fold_in(keys[9], part), 10)
    return {
        "pair": draw_pair(jax.random.fold_in(jax.random.fold_in(keys[9], part), 71), part),
        "residue_mask": touch_ends((jax.random.randint(own_keys[1], (N,), 0, 8) < 7).astype(jnp.int32), jax.random.fold_in(own_keys[1], 1), 0, 1),
        "ln_gain": jnp.clip(1.0 + 0.18 * jax.random.normal(keys[2], (2, C), jnp.float32), 0.1, 1.9),
        "ln_bias": draw_ln_bias(jax.random.fold_in(keys[9], 71), part),
        "w_ab": gaussian(keys[4], (2, C, 4 * CH), C ** -0.5, 0.5),
        "w_gate": gaussian(keys[5], (2, C, C), C ** -0.5, 0.5),
        "out_gain": draw_out_gain(jax.random.fold_in(keys[9], 71), part),
        "out_bias": gaussian(keys[7], (2, CH), 0.2, 1.0, jnp.float32),
        "w_out": draw_w_out(jax.random.fold_in(keys[9], 71), part),
    }


def layer_norm(v, gain, bias):
    mean = lax.optimization_barrier(jnp.mean(v, axis=-1, keepdims=True))
    centred = v - mean
    var = lax.optimization_barrier(jnp.mean(centred * centred, axis=-1, keepdims=True))
    return centred * jax.lax.rsqrt(var + 1e-05) * gain + bias

def one_update(z, pm, layer, ln_gain, ln_bias, w_ab, w_gate, out_gain, out_bias, w_out):
    zn = layer_norm(z.astype(jnp.float32), ln_gain[layer], ln_bias[layer]).astype(jnp.bfloat16)
    flat = zn.reshape(N * N, C)
    proj = jnp.dot(flat, w_ab[layer], preferred_element_type=jnp.float32).reshape(N, N, 4 * CH)
    mask3 = pm[:, :, None]
    left = (jax.nn.sigmoid(proj[..., :CH]) * proj[..., CH:2 * CH] * mask3).astype(jnp.bfloat16)
    right = (jax.nn.sigmoid(proj[..., 2 * CH:3 * CH]) * proj[..., 3 * CH:] * mask3).astype(jnp.bfloat16)
    gate = jax.nn.sigmoid(jnp.dot(flat, w_gate[layer], preferred_element_type=jnp.float32)).reshape(N, N, C)
    if layer == 0:
        x = jnp.einsum('ikc,jkc->ijc', left.astype(jnp.float32), right.astype(jnp.float32))
    else:
        x = jnp.einsum('kic,kjc->ijc', left.astype(jnp.float32), right.astype(jnp.float32))
    xn = layer_norm(x, out_gain[layer], out_bias[layer]).astype(jnp.bfloat16)
    delta = jnp.dot(xn.reshape(N * N, CH), w_out[layer], preferred_element_type=jnp.float32).reshape(N, N, C)
    return (z.astype(jnp.float32) + gate * delta).astype(jnp.bfloat16)

def reference(pair, residue_mask, ln_gain, ln_bias, w_ab, w_gate, out_gain, out_bias, w_out):
    maskf = residue_mask.astype(jnp.float32)
    pm = maskf[:, None] * maskf[None, :]
    first = one_update(pair, pm, 0, ln_gain, ln_bias, w_ab, w_gate, out_gain, out_bias, w_out)
    return one_update(first, pm, 1, ln_gain, ln_bias, w_ab, w_gate, out_gain, out_bias, w_out)
```

```python
import functools

import jax
import jax.numpy as jnp
from jax import lax
from jax.experimental import pallas as pl
from jax.experimental.pallas import tpu as pltpu
from jax.sharding import PartitionSpec as P


def from_root(value, axis, source):
    kept = jnp.where(lax.axis_index(axis) == source, value, 0).astype(value.dtype)
    return lax.psum(kept, axis)


def layer_norm(v, gain, bias):
    mean = jnp.mean(v, axis=-1, keepdims=True)
    centred = v - mean
    var = jnp.mean(centred * centred, axis=-1, keepdims=True)
    return centred * lax.rsqrt(var + 1e-05) * gain + bias


def project(z, pm, layer, ln_gain, ln_bias, w_ab, w_gate):
    rows, cols, chans = z.shape
    hidden = w_ab.shape[2] // 4
    zn = layer_norm(z.astype(jnp.float32), ln_gain[layer], ln_bias[layer]).astype(jnp.bfloat16)
    flat = zn.reshape(rows * cols, chans)
    proj = jnp.dot(flat, w_ab[layer], preferred_element_type=jnp.float32).reshape(
        rows, cols, 4 * hidden
    )
    mask3 = pm[:, :, None]
    left = (jax.nn.sigmoid(proj[..., :hidden]) * proj[..., hidden : 2 * hidden] * mask3).astype(
        jnp.bfloat16
    )
    right = (
        jax.nn.sigmoid(proj[..., 2 * hidden : 3 * hidden]) * proj[..., 3 * hidden :] * mask3
    ).astype(jnp.bfloat16)
    gate = jax.nn.sigmoid(jnp.dot(flat, w_gate[layer], preferred_element_type=jnp.float32)).reshape(
        rows, cols, chans
    )
    return (left, right, gate)


def finish(z, x, gate, layer, out_gain, out_bias, w_out):
    rows, cols, chans = z.shape
    hidden = x.shape[2]
    xn = layer_norm(x, out_gain[layer], out_bias[layer]).astype(jnp.bfloat16)
    delta = jnp.dot(
        xn.reshape(rows * cols, hidden), w_out[layer], preferred_element_type=jnp.float32
    )
    return (z.astype(jnp.float32) + gate * delta.reshape(rows, cols, chans)).astype(jnp.bfloat16)


def shards(pair, residue_mask, ln_gain, ln_bias, w_ab, w_gate, out_gain, out_bias, w_out):
    rows, cols, chans = pair.shape
    hidden = w_out.shape[1]
    row_count = lax.axis_size("row")
    total = rows * row_count
    row_pos = lax.axis_index("row")
    col_pos = lax.axis_index("col")
    maskf = residue_mask.astype(jnp.float32)
    mask_rows = lax.dynamic_slice_in_dim(maskf, row_pos * rows, rows)
    mask_cols = lax.dynamic_slice_in_dim(maskf, col_pos * cols, cols)
    pm = mask_rows[:, None] * mask_cols[None, :]
    left, right, gate = project(pair, pm, 0, ln_gain, ln_bias, w_ab, w_gate)
    left_flat = left.reshape(rows, cols * hidden)
    right_flat = right.reshape(rows, cols * hidden)
    left_wide, right_wide = (
        lax.all_gather(left_flat, "col", axis=1, tiled=True),
        lax.all_gather(right_flat, "col", axis=1, tiled=True),
    )
    left_full = left_wide.reshape(rows, total, hidden)
    piece = lax.all_gather(right_wide, "row", axis=0, tiled=True)
    count = piece.shape[0]
    contrib = jnp.einsum(
        "ikc,jkc->ijc",
        left_full,
        piece.reshape(count, total, hidden),
        preferred_element_type=jnp.float32,
    )
    outgoing = lax.dynamic_slice_in_dim(contrib, col_pos * cols, cols, 1)
    first = finish(pair, outgoing, gate, 0, out_gain, out_bias, w_out)
    left, right, gate = project(first, pm, 1, ln_gain, ln_bias, w_ab, w_gate)
    blocks_half = cols // rows
    left_blocks = left.reshape(rows, blocks_half, rows * hidden)
    padded = jnp.zeros((rows, row_count, rows * hidden), jnp.bfloat16)
    padded = lax.dynamic_update_slice_in_dim(padded, left_blocks, col_pos * blocks_half, 1)
    received = lax.all_to_all(padded, "row", split_axis=1, concat_axis=0, tiled=True)
    owner = row_pos * rows // cols
    left_cols = from_root(received, "col", owner).reshape(total, rows, hidden)
    piece = lax.all_gather(right.reshape(rows, cols * hidden), "row", axis=0, tiled=True)
    count = piece.shape[0]
    incoming = jnp.einsum(
        "kic,kjc->ijc",
        left_cols,
        piece.reshape(count, cols, hidden),
        preferred_element_type=jnp.float32,
    )
    return finish(first, incoming, gate, 1, out_gain, out_bias, w_out)


F32 = jnp.float32
BF16 = jnp.bfloat16
TILE = 8
LANES = 128


def sigmoid(v):
    return 0.5 * jnp.tanh(0.5 * v) + 0.5


def matmul(a, b, contract=((1,), (0,))):
    return lax.dot_general(a, b, (contract, ((), ())), preferred_element_type=F32)


def column(ref, layer):
    row = ref[layer : layer + 1, :]
    return jnp.transpose(jnp.broadcast_to(row, (row.shape[1], row.shape[1])))


def fused(
    count,
    pair_ref,
    mask_ref,
    mask_s,
    ln_gain,
    ln_bias,
    w_ab,
    w_gate,
    out_gain,
    out_bias,
    w_out,
    out_ref,
    z_t,
    zn_t,
    gate_t,
    stage,
    lr_out,
    lr_in,
    x_out,
    x_in,
    x_wide,
    lr_send,
    lr_recv,
    x_send,
    x_recv,
):
    rows, n, chans = pair_ref.shape
    hidden = w_out.shape[1]
    own = hidden // count
    per_lr = 2 * rows
    me = lax.axis_index("row")

    barrier = pltpu.get_barrier_semaphore()

    def greet(step, carry):
        other = lax.rem(me + step, count)
        pl.semaphore_signal(
            barrier, inc=1, device_id={"row": other}, device_id_type=pl.DeviceIdType.MESH
        )
        return carry

    lax.fori_loop(1, count, greet, 0)

    def lr_copy(u, slot_out, slot_in, other):
        return pltpu.make_async_remote_copy(
            src_ref=lr_out.at[u, slot_out],
            dst_ref=lr_in.at[u, slot_in],
            send_sem=lr_send.at[u, slot_out],
            recv_sem=lr_recv.at[u, slot_in],
            device_id={"row": other},
            device_id_type=pl.DeviceIdType.MESH,
        )

    def x_copy(u, slot_out, slot_in, other):
        return pltpu.make_async_remote_copy(
            src_ref=x_out.at[u, slot_out],
            dst_ref=x_in.at[u, slot_in],
            send_sem=x_send.at[u, slot_out],
            recv_sem=x_recv.at[u, slot_in],
            device_id={"row": other},
            device_id_type=pl.DeviceIdType.MESH,
        )

    mask_k = mask_ref[...].astype(F32)
    for i in range(rows):
        z_t[i] = jnp.transpose(pair_ref[i].astype(F32))

    for u in range(2):
        w_t = jnp.transpose(w_ab[u].astype(F32)).astype(BF16)
        gain, bias = column(ln_gain, u), column(ln_bias, u)
        for i in range(rows):
            z = z_t[i]
            mean = jnp.mean(z, axis=0, keepdims=True)
            centred = z - mean
            var = jnp.mean(centred * centred, axis=0, keepdims=True)
            zn = (centred * lax.rsqrt(var + 1e-05) * gain + bias).astype(BF16)
            zn_t[i] = zn
            proj = matmul(w_t, zn)
            pm = mask_k * mask_s[me * rows + i].astype(F32)
            left = sigmoid(proj[:hidden]) * proj[hidden : 2 * hidden] * pm
            right = sigmoid(proj[2 * hidden : 3 * hidden]) * proj[3 * hidden :] * pm
            stage[pl.ds(i, hidden, stride=per_lr), :] = left
            stage[pl.ds(rows + i, hidden, stride=per_lr), :] = right

        if u == 0:
            pl.semaphore_wait(barrier, count - 1)

        def lr_start(step, carry):
            other = lax.rem(me + step, count)
            begin = pl.multiple_of(other * (own * per_lr), own * per_lr)
            lr_out[u, other] = stage[pl.ds(begin, own * per_lr), :].astype(BF16)
            lr_copy(u, other, me, other).start()
            return carry

        lax.fori_loop(1, count, lr_start, 0)
        begin = pl.multiple_of(me * (own * per_lr), own * per_lr)
        lr_in[u, me] = stage[pl.ds(begin, own * per_lr), :].astype(BF16)

        w_gate_t = jnp.transpose(w_gate[u].astype(F32)).astype(BF16)
        for i in range(rows):
            gate_t[i] = sigmoid(matmul(w_gate_t, zn_t[i]))

        def lr_wait(step, carry):
            other = lax.rem(me + step, count)
            lr_copy(u, me, other, other).wait_recv()
            return carry

        lax.fori_loop(1, count, lr_wait, 0)

        for c in range(0, own, 2):
            found = []
            for d in range(c, c + 2):
                both = lr_in[u, :, d * per_lr : (d + 1) * per_lr, :].astype(F32)
                left = both[:, :rows].reshape(n, n).astype(BF16)
                right = both[:, rows:].reshape(n, n).astype(BF16)
                contract = ((1,), (1,)) if u == 0 else ((0,), (0,))
                found.append(matmul(left, right, contract).reshape(count, rows, n))
            x_out[u, :, c * rows : (c + 2) * rows, :] = jnp.concatenate(found, axis=1).astype(BF16)

        def x_start(step, carry):
            other = lax.rem(me + step, count)
            x_copy(u, other, me, other).start()
            return carry

        lax.fori_loop(1, count, x_start, 0)
        x_in[u, me] = x_out[u, me]

        w_out_t = jnp.transpose(w_out[u].astype(F32)).astype(BF16)
        gain, bias = column(out_gain, u), column(out_bias, u)

        def x_wait(step, carry):
            other = lax.rem(me + step, count)
            x_copy(u, me, other, other).wait_recv()
            return carry

        lax.fori_loop(1, count, x_wait, 0)

        x = x_in[u].astype(F32).reshape(hidden, rows, n)
        mean = jnp.mean(x, axis=0)
        centred = x - mean[None]
        var = jnp.mean(centred * centred, axis=0)
        x_wide[...] = (centred * lax.rsqrt(var + 1e-05)[None]).reshape(hidden * rows, n)
        for i in range(rows):
            xn = (x_wide[pl.ds(i, hidden, stride=rows), :] * gain + bias).astype(BF16)
            z = z_t[i] + gate_t[i] * matmul(w_out_t, xn)
            if u == 0:
                z_t[i] = z.astype(BF16).astype(F32)
            else:
                out_ref[i] = jnp.transpose(z).astype(BF16)

        def drain(step, carry):
            other = lax.rem(me + step, count)
            lr_copy(u, other, me, other).wait_send()
            x_copy(u, other, me, other).wait_send()
            return carry

        lax.fori_loop(1, count, drain, 0)


def fused_call(count, pair, residue_mask, *params):
    rows, n, chans = pair.shape
    hidden = params[-1].shape[1]
    own = hidden // count
    vmem = pl.BlockSpec(memory_space=pltpu.VMEM)
    return pl.pallas_call(
        functools.partial(fused, count),
        out_shape=jax.ShapeDtypeStruct(pair.shape, BF16),
        in_specs=[vmem, vmem, pl.BlockSpec(memory_space=pltpu.SMEM)] + [vmem] * 7,
        out_specs=vmem,
        scratch_shapes=[
            pltpu.VMEM((rows, chans, n), F32),
            pltpu.VMEM((rows, chans, n), BF16),
            pltpu.VMEM((rows, chans, n), F32),
            pltpu.VMEM((hidden * 2 * rows, n), F32),
            pltpu.VMEM((2, count, own * 2 * rows, n), BF16),
            pltpu.VMEM((2, count, own * 2 * rows, n), BF16),
            pltpu.VMEM((2, count, own * rows, n), BF16),
            pltpu.VMEM((2, count, own * rows, n), BF16),
            pltpu.VMEM((hidden * rows, n), F32),
            pltpu.SemaphoreType.DMA((2, count)),
            pltpu.SemaphoreType.DMA((2, count)),
            pltpu.SemaphoreType.DMA((2, count)),
            pltpu.SemaphoreType.DMA((2, count)),
        ],
        compiler_params=pltpu.CompilerParams(
            collective_id=0, has_side_effects=True, vmem_limit_bytes=48 * 1024 * 1024
        ),
        cost_estimate=pl.CostEstimate(
            flops=4 * rows * n * chans * (5 * hidden + n + hidden),
            bytes_accessed=4 * rows * n * chans,
            transcendentals=6 * rows * n * hidden,
        ),
    )(pair, residue_mask.reshape(1, n), residue_mask, *params)


def per_device(count, fits, pair, *rest):
    rows, cols, chans = pair.shape
    hidden = rest[-1].shape[1]
    if (
        fits
        and rows == TILE
        and cols == rows * count == LANES
        and chans == LANES
        and hidden == LANES
        and hidden % (2 * count) == 0
    ):
        return fused_call(count, pair, *rest)
    return shards(pair, *rest)


def solution(mesh):
    in_specs = (P(("group", "row"), "col", None), P("group"), P(), P(), P(), P(), P(), P(), P())
    out_specs = P(("group", "row"), "col", None)
    body = functools.partial(per_device, mesh.shape["row"], mesh.shape["col"] == 1)
    return jax.shard_map(body, mesh=mesh, in_specs=in_specs, out_specs=out_specs, check_vma=False)
```

```python
import functools

import jax
import jax.numpy as jnp
from jax import lax
from jax.experimental import pallas as pl
from jax.experimental.pallas import tpu as pltpu
from jax.sharding import PartitionSpec as P


def from_root(value, axis, source):
    kept = jnp.where(lax.axis_index(axis) == source, value, 0).astype(value.dtype)
    return lax.psum(kept, axis)


def layer_norm(v, gain, bias):
    mean = jnp.mean(v, axis=-1, keepdims=True)
    centred = v - mean
    var = jnp.mean(centred * centred, axis=-1, keepdims=True)
    return centred * lax.rsqrt(var + 1e-05) * gain + bias


def project(z, pm, layer, ln_gain, ln_bias, w_ab, w_gate):
    rows, cols, chans = z.shape
    hidden = w_ab.shape[2] // 4
    zn = layer_norm(z.astype(jnp.float32), ln_gain[layer], ln_bias[layer]).astype(jnp.bfloat16)
    flat = zn.reshape(rows * cols, chans)
    proj = jnp.dot(flat, w_ab[layer], preferred_element_type=jnp.float32).reshape(
        rows, cols, 4 * hidden
    )
    mask3 = pm[:, :, None]
    left = (jax.nn.sigmoid(proj[..., :hidden]) * proj[..., hidden : 2 * hidden] * mask3).astype(
        jnp.bfloat16
    )
    right = (
        jax.nn.sigmoid(proj[..., 2 * hidden : 3 * hidden]) * proj[..., 3 * hidden :] * mask3
    ).astype(jnp.bfloat16)
    gate = jax.nn.sigmoid(jnp.dot(flat, w_gate[layer], preferred_element_type=jnp.float32)).reshape(
        rows, cols, chans
    )
    return (left, right, gate)


def finish(z, x, gate, layer, out_gain, out_bias, w_out):
    rows, cols, chans = z.shape
    hidden = x.shape[2]
    xn = layer_norm(x, out_gain[layer], out_bias[layer]).astype(jnp.bfloat16)
    delta = jnp.dot(
        xn.reshape(rows * cols, hidden), w_out[layer], preferred_element_type=jnp.float32
    )
    return (z.astype(jnp.float32) + gate * delta.reshape(rows, cols, chans)).astype(jnp.bfloat16)


def shards(pair, residue_mask, ln_gain, ln_bias, w_ab, w_gate, out_gain, out_bias, w_out):
    rows, cols, chans = pair.shape
    hidden = w_out.shape[1]
    row_count = lax.axis_size("row")
    total = rows * row_count
    row_pos = lax.axis_index("row")
    col_pos = lax.axis_index("col")
    maskf = residue_mask.astype(jnp.float32)
    mask_rows = lax.dynamic_slice_in_dim(maskf, row_pos * rows, rows)
    mask_cols = lax.dynamic_slice_in_dim(maskf, col_pos * cols, cols)
    pm = mask_rows[:, None] * mask_cols[None, :]
    left, right, gate = project(pair, pm, 0, ln_gain, ln_bias, w_ab, w_gate)
    left_flat = left.reshape(rows, cols * hidden)
    right_flat = right.reshape(rows, cols * hidden)
    left_wide, right_wide = (
        lax.all_gather(left_flat, "col", axis=1, tiled=True),
        lax.all_gather(right_flat, "col", axis=1, tiled=True),
    )
    left_full = left_wide.reshape(rows, total, hidden)
    piece = lax.all_gather(right_wide, "row", axis=0, tiled=True)
    count = piece.shape[0]
    contrib = jnp.einsum(
        "ikc,jkc->ijc",
        left_full,
        piece.reshape(count, total, hidden),
        preferred_element_type=jnp.float32,
    )
    outgoing = lax.dynamic_slice_in_dim(contrib, col_pos * cols, cols, 1)
    first = finish(pair, outgoing, gate, 0, out_gain, out_bias, w_out)
    left, right, gate = project(first, pm, 1, ln_gain, ln_bias, w_ab, w_gate)
    blocks_half = cols // rows
    left_blocks = left.reshape(rows, blocks_half, rows * hidden)
    padded = jnp.zeros((rows, row_count, rows * hidden), jnp.bfloat16)
    padded = lax.dynamic_update_slice_in_dim(padded, left_blocks, col_pos * blocks_half, 1)
    received = lax.all_to_all(padded, "row", split_axis=1, concat_axis=0, tiled=True)
    owner = row_pos * rows // cols
    left_cols = from_root(received, "col", owner).reshape(total, rows, hidden)
    piece = lax.all_gather(right.reshape(rows, cols * hidden), "row", axis=0, tiled=True)
    count = piece.shape[0]
    incoming = jnp.einsum(
        "kic,kjc->ijc",
        left_cols,
        piece.reshape(count, cols, hidden),
        preferred_element_type=jnp.float32,
    )
    return finish(first, incoming, gate, 1, out_gain, out_bias, w_out)


F32 = jnp.float32
BF16 = jnp.bfloat16
TILE = 8
LANES = 128
PARTS = 1


def sigmoid(v):
    return 0.5 * jnp.tanh(0.5 * v) + 0.5


def matmul(a, b, contract=((1,), (0,))):
    return lax.dot_general(a, b, (contract, ((), ())), preferred_element_type=F32)


def column(ref, layer):
    row = ref[layer : layer + 1, :]
    return jnp.transpose(jnp.broadcast_to(row, (row.shape[1], row.shape[1])))


def fused(
    count,
    pair_hbm,
    mask_hbm,
    ln_gain_hbm,
    ln_bias_hbm,
    w_ab_hbm,
    w_gate_hbm,
    out_gain_hbm,
    out_bias_hbm,
    w_out_hbm,
    out_ref,
    pair_ref,
    mask_ref,
    ln_gain,
    ln_bias,
    w_ab,
    w_gate,
    out_gain,
    out_bias,
    w_out,
    load_sem,
    z_t,
    zn_t,
    gate_t,
    stage,
    lr_out,
    lr_in,
    x_out,
    x_in,
    x_wide,
    lr_send,
    lr_recv,
    x_send,
    x_recv,
):
    rows, n, chans = pair_ref.shape
    hidden = w_out.shape[1]
    half = hidden // PARTS
    own = half // count
    per_lr = 2 * rows
    wide = 2 * n
    me = lax.axis_index("row")

    held = (pair_ref, mask_ref, ln_gain, ln_bias, w_ab, w_gate, out_gain, out_bias, w_out)
    given = (
        pair_hbm,
        mask_hbm,
        ln_gain_hbm,
        ln_bias_hbm,
        w_ab_hbm,
        w_gate_hbm,
        out_gain_hbm,
        out_bias_hbm,
        w_out_hbm,
    )
    loads = [
        pltpu.make_async_copy(src, dst, load_sem.at[k])
        for k, (src, dst) in enumerate(zip(given, held))
    ]
    for load in loads:
        load.start()

    barrier = pltpu.get_barrier_semaphore()

    def greet(step, carry):
        other = lax.rem(me + step, count)
        pl.semaphore_signal(
            barrier, inc=1, device_id={"row": other}, device_id_type=pl.DeviceIdType.MESH
        )
        return carry

    lax.fori_loop(1, count, greet, 0, unroll=True)

    others = pl.ds(0, count - 1)

    def lr_copy(u, h, slot_out, slot_in, other):
        return pltpu.make_async_remote_copy(
            src_ref=lr_out.at[u, h, slot_out],
            dst_ref=lr_in.at[u, h, slot_in],
            send_sem=lr_send.at[u, h],
            recv_sem=lr_recv.at[u, h],
            device_id={"row": other},
            device_id_type=pl.DeviceIdType.MESH,
        )

    def x_copy(u, h, slot_out, slot_in, other):
        return pltpu.make_async_remote_copy(
            src_ref=x_out.at[u, h, slot_out],
            dst_ref=x_in.at[u, h, slot_in],
            send_sem=x_send.at[u, h],
            recv_sem=x_recv.at[u, h],
            device_id={"row": other},
            device_id_type=pl.DeviceIdType.MESH,
        )

    for load in loads:
        load.wait()
    mask_k = mask_ref[...].astype(F32)
    lane = lax.broadcasted_iota(jnp.int32, mask_k.shape, 1)
    masks = []
    for i in range(rows):
        mine = jnp.sum(jnp.where(lane == me * rows + i, mask_k, 0.0), axis=1, keepdims=True)
        masks.append(mask_k * mine)
    pm = [jnp.concatenate(masks[i : i + 2], axis=1) for i in range(0, rows, 2)]

    for u in range(2):
        w_t = jnp.transpose(w_ab[u].astype(F32)).astype(BF16)
        gain, bias = column(ln_gain, u), column(ln_bias, u)
        for i in range(rows):
            if u == 0:
                z_t[i] = jnp.transpose(pair_ref[i].astype(F32))
            z = z_t[i]
            mean = jnp.mean(z, axis=0, keepdims=True)
            centred = z - mean
            var = jnp.mean(centred * centred, axis=0, keepdims=True)
            zn = centred * lax.rsqrt(var + 1e-05) * gain + bias
            zn_t[:, i * n : (i + 1) * n] = zn.astype(BF16)

        for h in range(PARTS):
            w_h = jnp.concatenate(
                [w_t[p * hidden + h * half : p * hidden + (h + 1) * half] for p in range(4)], axis=0
            )
            for i in range(0, rows, 2):
                proj = matmul(w_h, zn_t[:, i * n : (i + 2) * n])
                left = sigmoid(proj[:half]) * proj[half : 2 * half] * pm[i // 2]
                right = sigmoid(proj[2 * half : 3 * half]) * proj[3 * half :] * pm[i // 2]
                for d in range(2):
                    at = h * half * per_lr + i + d
                    stage[pl.ds(at, half, stride=per_lr), :] = left[:, d * n : (d + 1) * n]
                    stage[pl.ds(at + rows, half, stride=per_lr), :] = right[:, d * n : (d + 1) * n]

            if u == 0 and h == 0:
                pl.semaphore_wait(barrier, count - 1)

            def block(other):
                begin = pl.multiple_of((h * half + other * own) * per_lr, own * per_lr)
                return stage[pl.ds(begin, own * per_lr), :].astype(BF16)

            def lr_start(step, carry):
                other = lax.rem(me + step, count)
                lr_out[u, h, other] = block(other)
                lr_copy(u, h, other, me, other).start()
                return carry

            lax.fori_loop(1, count, lr_start, 0, unroll=True)
            lr_in[u, h, me] = block(me)

        w_gate_t = jnp.transpose(w_gate[u].astype(F32)).astype(BF16)
        for i in range(0, rows, 2):
            at = slice(i * n, (i + 2) * n)
            gate_t[:, at] = sigmoid(matmul(w_gate_t, zn_t[:, at]))
        w_out_t = jnp.transpose(w_out[u].astype(F32)).astype(BF16)
        gain, bias = column(out_gain, u), column(out_bias, u)

        for h in range(PARTS):

            lr_copy(u, h, others, others, me).wait_recv()

            for c in range(0, own, 2):
                found = []
                for d in range(c, c + 2):
                    both = lr_in[u, h, :, d * per_lr : (d + 1) * per_lr, :].astype(F32)
                    left = both[:, :rows].reshape(n, n).astype(BF16)
                    right = both[:, rows:].reshape(n, n).astype(BF16)
                    contract = ((1,), (1,)) if u == 0 else ((0,), (0,))
                    found.append(matmul(left, right, contract).reshape(count, rows, n))
                x_out[u, h, :, c * rows : (c + 2) * rows, :] = jnp.concatenate(
                    found, axis=1
                ).astype(BF16)

            def x_start(step, carry):
                other = lax.rem(me + step, count)
                x_copy(u, h, other, me, other).start()
                return carry

            lax.fori_loop(1, count, x_start, 0, unroll=True)
            x_in[u, h, me] = x_out[u, h, me]

        for h in range(PARTS):

            x_copy(u, h, others, others, me).wait_recv()

        x = x_in[u].astype(F32).reshape(hidden, rows, n)
        mean = jnp.mean(x, axis=0)
        centred = x - mean[None]
        var = jnp.mean(centred * centred, axis=0)
        x_wide[...] = (centred * lax.rsqrt(var + 1e-05)[None]).reshape(hidden * rows, n)
        for i in range(0, rows, 2):
            xn = [
                (x_wide[pl.ds(i + d, hidden, stride=rows), :] * gain + bias).astype(BF16)
                for d in range(2)
            ]
            update = matmul(w_out_t, jnp.concatenate(xn, axis=1))
            update = gate_t[:, i * n : (i + 2) * n] * update
            for d in range(2):
                z = z_t[i + d] + update[:, d * n : (d + 1) * n]
                if u == 0:
                    z_t[i + d] = z.astype(BF16).astype(F32)
                else:
                    out_ref[i + d] = jnp.transpose(z).astype(BF16)

    for u in range(2):
        for h in range(PARTS):

            lr_copy(u, h, others, others, me).wait_send()
            x_copy(u, h, others, others, me).wait_send()


def fused_call(count, pair, residue_mask, *params):
    rows, n, chans = pair.shape
    hidden = params[-1].shape[1]
    own = hidden // PARTS // count
    args = (pair, residue_mask.reshape(1, n)) + params
    return pl.pallas_call(
        functools.partial(fused, count),
        out_shape=jax.ShapeDtypeStruct(pair.shape, BF16),
        in_specs=[pl.BlockSpec(memory_space=pltpu.HBM)] * len(args),
        out_specs=pl.BlockSpec(memory_space=pltpu.VMEM),
        scratch_shapes=[pltpu.VMEM(a.shape, a.dtype) for a in args]
        + [
            pltpu.SemaphoreType.DMA((len(args),)),
            pltpu.VMEM((rows, chans, n), F32),
            pltpu.VMEM((chans, rows * n), BF16),
            pltpu.VMEM((chans, rows * n), F32),
            pltpu.VMEM((hidden * 2 * rows, n), F32),
            pltpu.VMEM((2, PARTS, count, own * 2 * rows, n), BF16),
            pltpu.VMEM((2, PARTS, count, own * 2 * rows, n), BF16),
            pltpu.VMEM((2, PARTS, count, own * rows, n), BF16),
            pltpu.VMEM((2, PARTS, count, own * rows, n), BF16),
            pltpu.VMEM((hidden * rows, n), F32),
            pltpu.SemaphoreType.DMA((2, PARTS)),
            pltpu.SemaphoreType.DMA((2, PARTS)),
            pltpu.SemaphoreType.DMA((2, PARTS)),
            pltpu.SemaphoreType.DMA((2, PARTS)),
        ],
        compiler_params=pltpu.CompilerParams(
            collective_id=0, has_side_effects=True, vmem_limit_bytes=63 * 1024 * 1024
        ),
        cost_estimate=pl.CostEstimate(
            flops=4 * rows * n * chans * (5 * hidden + n + hidden),
            bytes_accessed=4 * rows * n * chans,
            transcendentals=6 * rows * n * hidden,
        ),
    )(*args)


def per_device(count, fits, pair, *rest):
    rows, cols, chans = pair.shape
    hidden = rest[-1].shape[1]
    if (
        fits
        and rows == TILE
        and cols == rows * count == LANES
        and chans == LANES
        and hidden == LANES
        and hidden % (2 * PARTS * count) == 0
    ):
        return fused_call(count, pair, *rest)
    return shards(pair, *rest)


def solution(mesh):
    in_specs = (P(("group", "row"), "col", None), P("group"), P(), P(), P(), P(), P(), P(), P())
    out_specs = P(("group", "row"), "col", None)
    body = functools.partial(per_device, mesh.shape["row"], mesh.shape["col"] == 1)
    return jax.shard_map(body, mesh=mesh, in_specs=in_specs, out_specs=out_specs, check_vma=False)
```

```python
import functools

import jax
import jax.numpy as jnp
from jax import lax
from jax.experimental import pallas as pl
from jax.experimental.pallas import tpu as pltpu
from jax.sharding import PartitionSpec as P


def from_root(value, axis, source):
    kept = jnp.where(lax.axis_index(axis) == source, value, 0).astype(value.dtype)
    return lax.psum(kept, axis)


def layer_norm(v, gain, bias):
    mean = jnp.mean(v, axis=-1, keepdims=True)
    centred = v - mean
    var = jnp.mean(centred * centred, axis=-1, keepdims=True)
    return centred * lax.rsqrt(var + 1e-05) * gain + bias


def project(z, pm, layer, ln_gain, ln_bias, w_ab, w_gate):
    rows, cols, chans = z.shape
    hidden = w_ab.shape[2] // 4
    zn = layer_norm(z.astype(jnp.float32), ln_gain[layer], ln_bias[layer]).astype(jnp.bfloat16)
    flat = zn.reshape(rows * cols, chans)
    proj = jnp.dot(flat, w_ab[layer], preferred_element_type=jnp.float32).reshape(
        rows, cols, 4 * hidden
    )
    mask3 = pm[:, :, None]
    left = (jax.nn.sigmoid(proj[..., :hidden]) * proj[..., hidden : 2 * hidden] * mask3).astype(
        jnp.bfloat16
    )
    right = (
        jax.nn.sigmoid(proj[..., 2 * hidden : 3 * hidden]) * proj[..., 3 * hidden :] * mask3
    ).astype(jnp.bfloat16)
    gate = jax.nn.sigmoid(jnp.dot(flat, w_gate[layer], preferred_element_type=jnp.float32)).reshape(
        rows, cols, chans
    )
    return (left, right, gate)


def finish(z, x, gate, layer, out_gain, out_bias, w_out):
    rows, cols, chans = z.shape
    hidden = x.shape[2]
    xn = layer_norm(x, out_gain[layer], out_bias[layer]).astype(jnp.bfloat16)
    delta = jnp.dot(
        xn.reshape(rows * cols, hidden), w_out[layer], preferred_element_type=jnp.float32
    )
    return (z.astype(jnp.float32) + gate * delta.reshape(rows, cols, chans)).astype(jnp.bfloat16)


def shards(pair, residue_mask, ln_gain, ln_bias, w_ab, w_gate, out_gain, out_bias, w_out):
    rows, cols, chans = pair.shape
    hidden = w_out.shape[1]
    row_count = lax.axis_size("row")
    total = rows * row_count
    row_pos = lax.axis_index("row")
    col_pos = lax.axis_index("col")
    maskf = residue_mask.astype(jnp.float32)
    mask_rows = lax.dynamic_slice_in_dim(maskf, row_pos * rows, rows)
    mask_cols = lax.dynamic_slice_in_dim(maskf, col_pos * cols, cols)
    pm = mask_rows[:, None] * mask_cols[None, :]
    left, right, gate = project(pair, pm, 0, ln_gain, ln_bias, w_ab, w_gate)
    left_flat = left.reshape(rows, cols * hidden)
    right_flat = right.reshape(rows, cols * hidden)
    left_wide, right_wide = (
        lax.all_gather(left_flat, "col", axis=1, tiled=True),
        lax.all_gather(right_flat, "col", axis=1, tiled=True),
    )
    left_full = left_wide.reshape(rows, total, hidden)
    piece = lax.all_gather(right_wide, "row", axis=0, tiled=True)
    count = piece.shape[0]
    contrib = jnp.einsum(
        "ikc,jkc->ijc",
        left_full,
        piece.reshape(count, total, hidden),
        preferred_element_type=jnp.float32,
    )
    outgoing = lax.dynamic_slice_in_dim(contrib, col_pos * cols, cols, 1)
    first = finish(pair, outgoing, gate, 0, out_gain, out_bias, w_out)
    left, right, gate = project(first, pm, 1, ln_gain, ln_bias, w_ab, w_gate)
    blocks_half = cols // rows
    left_blocks = left.reshape(rows, blocks_half, rows * hidden)
    padded = jnp.zeros((rows, row_count, rows * hidden), jnp.bfloat16)
    padded = lax.dynamic_update_slice_in_dim(padded, left_blocks, col_pos * blocks_half, 1)
    received = lax.all_to_all(padded, "row", split_axis=1, concat_axis=0, tiled=True)
    owner = row_pos * rows // cols
    left_cols = from_root(received, "col", owner).reshape(total, rows, hidden)
    piece = lax.all_gather(right.reshape(rows, cols * hidden), "row", axis=0, tiled=True)
    count = piece.shape[0]
    incoming = jnp.einsum(
        "kic,kjc->ijc",
        left_cols,
        piece.reshape(count, cols, hidden),
        preferred_element_type=jnp.float32,
    )
    return finish(first, incoming, gate, 1, out_gain, out_bias, w_out)


F32 = jnp.float32
BF16 = jnp.bfloat16
TILE = 8
LANES = 128


def sigmoid(v):
    return 0.5 * jnp.tanh(0.5 * v) + 0.5


def matmul(a, b, contract=((1,), (0,))):
    return lax.dot_general(a, b, (contract, ((), ())), preferred_element_type=F32)


def column(ref, layer):
    row = ref[layer : layer + 1, :]
    return jnp.transpose(jnp.broadcast_to(row, (row.shape[1], row.shape[1])))


def fused(
    count,
    pair_hbm,
    mask_hbm,
    ln_gain_hbm,
    ln_bias_hbm,
    w_ab_hbm,
    w_gate_hbm,
    out_gain_hbm,
    out_bias_hbm,
    w_out_hbm,
    out_ref,
    pair_ref,
    mask_ref,
    ln_gain,
    ln_bias,
    w_ab,
    w_gate,
    out_gain,
    out_bias,
    w_out,
    load_sem,
    z_t,
    zn_t,
    gate_t,
    stage,
    w_next,
    edges,
    l_in0,
    r_in0,
    l_in1,
    r_in1,
    x_out0,
    x_out1,
    x_in0,
    x_in1,
    x_wide,
    l_send,
    l_recv,
    r_send,
    r_recv,
    x_send,
    x_recv,
):
    rows, n, chans = pair_ref.shape
    hidden = w_out.shape[1]
    l_in, r_in = (l_in0, l_in1), (r_in0, r_in1)
    x_out, x_in = (x_out0, x_out1), (x_in0, x_in1)
    me = lax.axis_index("row")

    held = (pair_ref, mask_ref, ln_gain, ln_bias, w_ab, w_gate, out_gain, out_bias, w_out)
    given = (
        pair_hbm,
        mask_hbm,
        ln_gain_hbm,
        ln_bias_hbm,
        w_ab_hbm,
        w_gate_hbm,
        out_gain_hbm,
        out_bias_hbm,
        w_out_hbm,
    )
    loads = [
        pltpu.make_async_copy(src, dst, load_sem.at[k])
        for k, (src, dst) in enumerate(zip(given, held))
    ]
    for load in loads:
        load.start()

    barrier = pltpu.get_barrier_semaphore()

    def greet(step, carry):
        other = lax.rem(me + step, count)
        pl.semaphore_signal(
            barrier, inc=1, device_id={"row": other}, device_id_type=pl.DeviceIdType.MESH
        )
        return carry

    lax.fori_loop(1, count, greet, 0, unroll=True)

    def send(src, dst, send_sem, recv_sem, other):
        return pltpu.make_async_remote_copy(
            src_ref=src,
            dst_ref=dst,
            send_sem=send_sem,
            recv_sem=recv_sem,
            device_id={"row": other},
            device_id_type=pl.DeviceIdType.MESH,
        )

    def all_blocks(u, kind):
        ref, send_sem, recv_sem = {
            "l": (l_in[u], l_send, l_recv),
            "r": (r_in[u], r_send, r_recv),
            "x": (x_in[u], x_send, x_recv),
        }[kind]
        blocks = ref.at[pl.ds(0, ref.shape[0] - 1)]
        return send(blocks, blocks, send_sem.at[u], recv_sem.at[u], me)

    for load in loads:
        load.wait()
    mask_k = mask_ref[...].astype(F32)
    lane = lax.broadcasted_iota(jnp.int32, mask_k.shape, 1)
    masks = []
    for i in range(rows):
        mine = jnp.sum(jnp.where(lane == me * rows + i, mask_k, 0.0), axis=1, keepdims=True)
        masks.append(mask_k * mine)
    pm = [jnp.concatenate(masks[i : i + 2], axis=1) for i in range(0, rows, 2)]

    for u in range(2):
        team = count // 2 if u == 0 else count
        own = hidden // team
        size = own * rows
        member = lax.rem(me, team)
        base = me - member
        if u == 0:
            w_t = jnp.transpose(w_ab[u].astype(F32)).astype(BF16)
        else:
            w_t = w_next[...]
        gain, bias = column(ln_gain, u), column(ln_bias, u)
        for i in range(rows):
            if u == 0:
                z_t[i] = jnp.transpose(pair_ref[i].astype(F32))
            z = z_t[i]
            mean = jnp.mean(z, axis=0, keepdims=True)
            centred = z - mean
            var = jnp.mean(centred * centred, axis=0, keepdims=True)
            zn = centred * lax.rsqrt(var + 1e-05) * gain + bias
            zn_t[:, i * n : (i + 1) * n] = zn.astype(BF16)

        for i in range(0, rows, 2):
            proj = matmul(w_t, zn_t[:, i * n : (i + 2) * n])
            left = sigmoid(proj[:hidden]) * proj[hidden : 2 * hidden] * pm[i // 2]
            right = sigmoid(proj[2 * hidden : 3 * hidden]) * proj[3 * hidden :] * pm[i // 2]
            for d in range(2):
                at = slice(d * n, (d + 1) * n)
                stage[pl.ds(i + d, hidden, stride=rows), :] = left[:, at]
                stage[pl.ds(hidden * rows + i + d, hidden, stride=rows), :] = right[:, at]
        edges[u, 0] = stage[: hidden * rows, :].astype(BF16)
        edges[u, 1] = stage[hidden * rows :, :].astype(BF16)

        if u == 0:
            pl.semaphore_wait(barrier, count - 1)

        def block(side, device):
            begin = pl.multiple_of(lax.rem(device, team) * size, size)
            return edges.at[u, side, pl.ds(begin, size)]

        for step in range(1, count):
            other = lax.rem(me + step, count)
            send(block(1, other), r_in[u].at[me], r_send.at[u], r_recv.at[u], other).start()
            if step < team:
                other = base + lax.rem(member + step, team)
                send(block(0, other), l_in[u].at[member], l_send.at[u], l_recv.at[u], other).start()
        r_in[u][me] = block(1, me)[...]
        l_in[u][member] = block(0, me)[...]

        w_gate_t = jnp.transpose(w_gate[u].astype(F32)).astype(BF16)
        for i in range(0, rows, 2):
            at = slice(i * n, (i + 2) * n)
            gate_t[:, at] = sigmoid(matmul(w_gate_t, zn_t[:, at]))
        w_out_t = jnp.transpose(w_out[u].astype(F32)).astype(BF16)
        gain, bias = column(out_gain, u), column(out_bias, u)
        if u == 0:
            w_next[...] = jnp.transpose(w_ab[1].astype(F32)).astype(BF16)

        all_blocks(u, "l").wait_recv()
        all_blocks(u, "r").wait_recv()
        for c in range(0, own, 2):
            at = slice(c * rows, (c + 2) * rows)
            lefts = l_in[u][:, at, :].astype(F32)
            rights = r_in[u][:, at, :].astype(F32)
            found = []
            for d in range(2):
                at_d = slice(d * rows, (d + 1) * rows)
                left = lefts[:, at_d].reshape(team * rows, n).astype(BF16)
                right = rights[:, at_d].reshape(n, n).astype(BF16)
                contract = ((1,), (1,)) if u == 0 else ((0,), (0,))
                found.append(matmul(left, right, contract).reshape(team, rows, n))
            x_out[u][:, at, :] = jnp.concatenate(found, axis=1).astype(BF16)

        for step in range(1, team):
            to = lax.rem(member + step, team)
            send(
                x_out[u].at[to], x_in[u].at[member], x_send.at[u], x_recv.at[u], base + to
            ).start()
        x_in[u][member] = x_out[u][member]
        all_blocks(u, "x").wait_recv()

        x = x_in[u][...].astype(F32).reshape(hidden, rows, n)
        mean = jnp.mean(x, axis=0)
        centred = x - mean[None]
        var = jnp.mean(centred * centred, axis=0)
        x_wide[...] = (centred * lax.rsqrt(var + 1e-05)[None]).reshape(hidden * rows, n)
        for i in range(0, rows, 2):
            xn = [
                (x_wide[pl.ds(i + d, hidden, stride=rows), :] * gain + bias).astype(BF16)
                for d in range(2)
            ]
            update = matmul(w_out_t, jnp.concatenate(xn, axis=1))
            update = gate_t[:, i * n : (i + 2) * n] * update
            for d in range(2):
                z = z_t[i + d] + update[:, d * n : (d + 1) * n]
                if u == 0:
                    z_t[i + d] = z.astype(BF16).astype(F32)
                else:
                    out_ref[i + d] = jnp.transpose(z).astype(BF16)

    for u in range(2):
        for kind in ("l", "r", "x"):
            all_blocks(u, kind).wait_send()


def fused_call(count, pair, residue_mask, *params):
    rows, n, chans = pair.shape
    hidden = params[-1].shape[1]
    per = rows * hidden // count
    args = (pair, residue_mask.reshape(1, n)) + params
    return pl.pallas_call(
        functools.partial(fused, count),
        out_shape=jax.ShapeDtypeStruct(pair.shape, BF16),
        in_specs=[pl.BlockSpec(memory_space=pltpu.HBM)] * len(args),
        out_specs=pl.BlockSpec(memory_space=pltpu.VMEM),
        scratch_shapes=[pltpu.VMEM(a.shape, a.dtype) for a in args]
        + [
            pltpu.SemaphoreType.DMA((len(args),)),
            pltpu.VMEM((rows, chans, n), F32),
            pltpu.VMEM((chans, rows * n), BF16),
            pltpu.VMEM((chans, rows * n), F32),
            pltpu.VMEM((hidden * 2 * rows, n), F32),
            pltpu.VMEM((4 * hidden, chans), BF16),
            pltpu.VMEM((2, 2, hidden * rows, n), BF16),
            pltpu.VMEM((count // 2, 2 * per, n), BF16),
            pltpu.VMEM((count, 2 * per, n), BF16),
            pltpu.VMEM((count, per, n), BF16),
            pltpu.VMEM((count, per, n), BF16),
            pltpu.VMEM((count // 2, 2 * per, n), BF16),
            pltpu.VMEM((count, per, n), BF16),
            pltpu.VMEM((count // 2, 2 * per, n), BF16),
            pltpu.VMEM((count, per, n), BF16),
            pltpu.VMEM((hidden * rows, n), F32),
            pltpu.SemaphoreType.DMA((2,)),
            pltpu.SemaphoreType.DMA((2,)),
            pltpu.SemaphoreType.DMA((2,)),
            pltpu.SemaphoreType.DMA((2,)),
            pltpu.SemaphoreType.DMA((2,)),
            pltpu.SemaphoreType.DMA((2,)),
        ],
        compiler_params=pltpu.CompilerParams(
            collective_id=0, has_side_effects=True, vmem_limit_bytes=63 * 1024 * 1024
        ),
        cost_estimate=pl.CostEstimate(
            flops=4 * rows * n * chans * (5 * hidden + n + hidden),
            bytes_accessed=4 * rows * n * chans,
            transcendentals=6 * rows * n * hidden,
        ),
    )(*args)


def per_device(count, fits, pair, *rest):
    rows, cols, chans = pair.shape
    hidden = rest[-1].shape[1]
    if (
        fits
        and rows == TILE
        and cols == rows * count == LANES
        and chans == LANES
        and hidden == LANES
        and hidden % (2 * count) == 0
        and count % 2 == 0
    ):
        return fused_call(count, pair, *rest)
    return shards(pair, *rest)


def solution(mesh):
    in_specs = (P(("group", "row"), "col", None), P("group"), P(), P(), P(), P(), P(), P(), P())
    out_specs = P(("group", "row"), "col", None)
    body = functools.partial(per_device, mesh.shape["row"], mesh.shape["col"] == 1)
    return jax.shard_map(body, mesh=mesh, in_specs=in_specs, out_specs=out_specs, check_vma=False)
```

```python
import functools

import jax
import jax.numpy as jnp
from jax import lax
from jax.experimental import pallas as pl
from jax.experimental.pallas import tpu as pltpu
from jax.sharding import PartitionSpec as P


def from_root(value, axis, source):
    kept = jnp.where(lax.axis_index(axis) == source, value, 0).astype(value.dtype)
    return lax.psum(kept, axis)


def layer_norm(v, gain, bias):
    mean = jnp.mean(v, axis=-1, keepdims=True)
    centred = v - mean
    var = jnp.mean(centred * centred, axis=-1, keepdims=True)
    return centred * lax.rsqrt(var + 1e-05) * gain + bias


def project(z, pm, layer, ln_gain, ln_bias, w_ab, w_gate):
    rows, cols, chans = z.shape
    hidden = w_ab.shape[2] // 4
    zn = layer_norm(z.astype(jnp.float32), ln_gain[layer], ln_bias[layer]).astype(jnp.bfloat16)
    flat = zn.reshape(rows * cols, chans)
    proj = jnp.dot(flat, w_ab[layer], preferred_element_type=jnp.float32).reshape(
        rows, cols, 4 * hidden
    )
    mask3 = pm[:, :, None]
    left = (jax.nn.sigmoid(proj[..., :hidden]) * proj[..., hidden : 2 * hidden] * mask3).astype(
        jnp.bfloat16
    )
    right = (
        jax.nn.sigmoid(proj[..., 2 * hidden : 3 * hidden]) * proj[..., 3 * hidden :] * mask3
    ).astype(jnp.bfloat16)
    gate = jax.nn.sigmoid(jnp.dot(flat, w_gate[layer], preferred_element_type=jnp.float32)).reshape(
        rows, cols, chans
    )
    return (left, right, gate)


def finish(z, x, gate, layer, out_gain, out_bias, w_out):
    rows, cols, chans = z.shape
    hidden = x.shape[2]
    xn = layer_norm(x, out_gain[layer], out_bias[layer]).astype(jnp.bfloat16)
    delta = jnp.dot(
        xn.reshape(rows * cols, hidden), w_out[layer], preferred_element_type=jnp.float32
    )
    return (z.astype(jnp.float32) + gate * delta.reshape(rows, cols, chans)).astype(jnp.bfloat16)


def shards(pair, residue_mask, ln_gain, ln_bias, w_ab, w_gate, out_gain, out_bias, w_out):
    rows, cols, chans = pair.shape
    hidden = w_out.shape[1]
    row_count = lax.axis_size("row")
    total = rows * row_count
    row_pos = lax.axis_index("row")
    col_pos = lax.axis_index("col")
    maskf = residue_mask.astype(jnp.float32)
    mask_rows = lax.dynamic_slice_in_dim(maskf, row_pos * rows, rows)
    mask_cols = lax.dynamic_slice_in_dim(maskf, col_pos * cols, cols)
    pm = mask_rows[:, None] * mask_cols[None, :]
    left, right, gate = project(pair, pm, 0, ln_gain, ln_bias, w_ab, w_gate)
    left_flat = left.reshape(rows, cols * hidden)
    right_flat = right.reshape(rows, cols * hidden)
    left_wide, right_wide = (
        lax.all_gather(left_flat, "col", axis=1, tiled=True),
        lax.all_gather(right_flat, "col", axis=1, tiled=True),
    )
    left_full = left_wide.reshape(rows, total, hidden)
    piece = lax.all_gather(right_wide, "row", axis=0, tiled=True)
    count = piece.shape[0]
    contrib = jnp.einsum(
        "ikc,jkc->ijc",
        left_full,
        piece.reshape(count, total, hidden),
        preferred_element_type=jnp.float32,
    )
    outgoing = lax.dynamic_slice_in_dim(contrib, col_pos * cols, cols, 1)
    first = finish(pair, outgoing, gate, 0, out_gain, out_bias, w_out)
    left, right, gate = project(first, pm, 1, ln_gain, ln_bias, w_ab, w_gate)
    blocks_half = cols // rows
    left_blocks = left.reshape(rows, blocks_half, rows * hidden)
    padded = jnp.zeros((rows, row_count, rows * hidden), jnp.bfloat16)
    padded = lax.dynamic_update_slice_in_dim(padded, left_blocks, col_pos * blocks_half, 1)
    received = lax.all_to_all(padded, "row", split_axis=1, concat_axis=0, tiled=True)
    owner = row_pos * rows // cols
    left_cols = from_root(received, "col", owner).reshape(total, rows, hidden)
    piece = lax.all_gather(right.reshape(rows, cols * hidden), "row", axis=0, tiled=True)
    count = piece.shape[0]
    incoming = jnp.einsum(
        "kic,kjc->ijc",
        left_cols,
        piece.reshape(count, cols, hidden),
        preferred_element_type=jnp.float32,
    )
    return finish(first, incoming, gate, 1, out_gain, out_bias, w_out)


F32 = jnp.float32
BF16 = jnp.bfloat16
TILE = 8
LANES = 128


def sigmoid(v):
    return 0.5 * jnp.tanh(0.5 * v) + 0.5


def matmul(a, b, contract=((1,), (0,))):
    return lax.dot_general(a, b, (contract, ((), ())), preferred_element_type=F32)


def column(ref, layer):
    row = ref[layer : layer + 1, :]
    return jnp.transpose(jnp.broadcast_to(row, (row.shape[1], row.shape[1])))


def fused(
    count,
    pair_hbm,
    mask_hbm,
    ln_gain_hbm,
    ln_bias_hbm,
    w_ab_hbm,
    w_gate_hbm,
    out_gain_hbm,
    out_bias_hbm,
    w_out_hbm,
    out_ref,
    pair_ref,
    mask_ref,
    ln_gain,
    ln_bias,
    w_ab,
    w_gate,
    out_gain,
    out_bias,
    w_out,
    load_sem,
    z_t,
    zn_t,
    gate_t,
    stage,
    w_next,
    edges0,
    edges1,
    in0,
    in1,
    x_out0,
    x_out1,
    x_in0,
    x_in1,
    x_wide,
    near_send,
    near_recv,
    far_send,
    far_recv,
    x_send,
    x_recv,
):
    rows, n, chans = pair_ref.shape
    hidden = w_out.shape[1]
    edges, edges_in = (edges0, edges1), (in0, in1)
    x_out, x_in = (x_out0, x_out1), (x_in0, x_in1)
    me = lax.axis_index("row")

    held = (pair_ref, mask_ref, ln_gain, ln_bias, w_ab, w_gate, out_gain, out_bias, w_out)
    given = (
        pair_hbm,
        mask_hbm,
        ln_gain_hbm,
        ln_bias_hbm,
        w_ab_hbm,
        w_gate_hbm,
        out_gain_hbm,
        out_bias_hbm,
        w_out_hbm,
    )
    loads = [
        pltpu.make_async_copy(src, dst, load_sem.at[k])
        for k, (src, dst) in enumerate(zip(given, held))
    ]
    for load in loads:
        load.start()

    barrier = pltpu.get_barrier_semaphore()

    def greet(step, carry):
        other = lax.rem(me + step, count)
        pl.semaphore_signal(
            barrier, inc=1, device_id={"row": other}, device_id_type=pl.DeviceIdType.MESH
        )
        return carry

    lax.fori_loop(1, count, greet, 0, unroll=True)

    def send(src, dst, send_sem, recv_sem, other):
        return pltpu.make_async_remote_copy(
            src_ref=src,
            dst_ref=dst,
            send_sem=send_sem,
            recv_sem=recv_sem,
            device_id={"row": other},
            device_id_type=pl.DeviceIdType.MESH,
        )

    def all_blocks(u, kind):
        if kind == "x":
            blocks = x_in[u].at[pl.ds(0, x_in[u].shape[0] - 1)]
            return send(blocks, blocks, x_send.at[u], x_recv.at[u], me)
        if kind == "near":
            blocks = edges_in[u].at[pl.ds(0, edges[u].shape[0] - 1)]
            return send(blocks, blocks, near_send.at[u], near_recv.at[u], me)
        blocks = edges_in[u].at[pl.ds(0, count - edges[u].shape[0]), 1]
        return send(blocks, blocks, far_send, far_recv, me)

    for load in loads:
        load.wait()
    mask_k = mask_ref[...].astype(F32)
    lane = lax.broadcasted_iota(jnp.int32, mask_k.shape, 1)
    masks = []
    for i in range(rows):
        mine = jnp.sum(jnp.where(lane == me * rows + i, mask_k, 0.0), axis=1, keepdims=True)
        masks.append(mask_k * mine)
    pm = [jnp.concatenate(masks[i : i + 2], axis=1) for i in range(0, rows, 2)]

    for u in range(2):
        team = count // 2 if u == 0 else count
        own = hidden // team
        size = own * rows
        member = lax.rem(me, team)
        base = me - member
        if u == 0:
            w_t = jnp.transpose(w_ab[u].astype(F32)).astype(BF16)
        else:
            w_t = w_next[...]
        gain, bias = column(ln_gain, u), column(ln_bias, u)
        for i in range(rows):
            if u == 0:
                z_t[i] = jnp.transpose(pair_ref[i].astype(F32))
            z = z_t[i]
            mean = jnp.mean(z, axis=0, keepdims=True)
            centred = z - mean
            var = jnp.mean(centred * centred, axis=0, keepdims=True)
            zn = centred * lax.rsqrt(var + 1e-05) * gain + bias
            zn_t[:, i * n : (i + 1) * n] = zn.astype(BF16)

        for i in range(0, rows, 2):
            proj = matmul(w_t, zn_t[:, i * n : (i + 2) * n])
            left = sigmoid(proj[:hidden]) * proj[hidden : 2 * hidden] * pm[i // 2]
            right = sigmoid(proj[2 * hidden : 3 * hidden]) * proj[3 * hidden :] * pm[i // 2]
            for d in range(2):
                at = slice(d * n, (d + 1) * n)
                stage[pl.ds(i + d, hidden, stride=rows), :] = left[:, at]
                stage[pl.ds(hidden * rows + i + d, hidden, stride=rows), :] = right[:, at]
        half = hidden * rows
        edges[u][:, 0] = stage[:half, :].astype(BF16).reshape(team, size, n)
        edges[u][:, 1] = stage[half:, :].astype(BF16).reshape(team, size, n)

        if u == 0:
            pl.semaphore_wait(barrier, count - 1)

        for step in range(1, team):
            to = lax.rem(member + step, team)
            near = edges_in[u].at[me]
            send(edges[u].at[to], near, near_send.at[u], near_recv.at[u], base + to).start()
            if team < count:
                to = lax.rem(member + step, team)
                far = edges_in[u].at[me, 1]
                other = lax.rem(base + team + to, count)
                send(edges[u].at[to, 1], far, far_send, far_recv, other).start()
        if team < count:
            far = edges_in[u].at[me, 1]
            other = lax.rem(me + team, count)
            send(edges[u].at[member, 1], far, far_send, far_recv, other).start()
        edges_in[u][me] = edges[u][member]

        w_gate_t = jnp.transpose(w_gate[u].astype(F32)).astype(BF16)
        for i in range(0, rows, 2):
            at = slice(i * n, (i + 2) * n)
            gate_t[:, at] = sigmoid(matmul(w_gate_t, zn_t[:, at]))
        w_out_t = jnp.transpose(w_out[u].astype(F32)).astype(BF16)
        gain, bias = column(out_gain, u), column(out_bias, u)
        if u == 0:
            w_next[...] = jnp.transpose(w_ab[1].astype(F32)).astype(BF16)

        all_blocks(u, "near").wait_recv()
        if team < count:
            all_blocks(u, "far").wait_recv()
        for c in range(0, own, 2):
            at = slice(c * rows, (c + 2) * rows)
            lefts = edges_in[u][pl.ds(base, team), 0, at, :].astype(F32)
            rights = edges_in[u][:, 1, at, :].astype(F32)
            found = []
            for d in range(2):
                at_d = slice(d * rows, (d + 1) * rows)
                left = lefts[:, at_d].reshape(team * rows, n).astype(BF16)
                right = rights[:, at_d].reshape(n, n).astype(BF16)
                contract = ((1,), (1,)) if u == 0 else ((0,), (0,))
                found.append(matmul(left, right, contract).reshape(team, rows, n))
            x_out[u][:, at, :] = jnp.concatenate(found, axis=1).astype(BF16)

        for step in range(1, team):
            to = lax.rem(member + step, team)
            send(
                x_out[u].at[to], x_in[u].at[member], x_send.at[u], x_recv.at[u], base + to
            ).start()
        x_in[u][member] = x_out[u][member]
        all_blocks(u, "x").wait_recv()

        x = x_in[u][...].astype(F32).reshape(hidden, rows, n)
        mean = jnp.mean(x, axis=0)
        centred = x - mean[None]
        var = jnp.mean(centred * centred, axis=0)
        x_wide[...] = (centred * lax.rsqrt(var + 1e-05)[None]).reshape(hidden * rows, n)
        for i in range(0, rows, 2):
            xn = [
                (x_wide[pl.ds(i + d, hidden, stride=rows), :] * gain + bias).astype(BF16)
                for d in range(2)
            ]
            update = matmul(w_out_t, jnp.concatenate(xn, axis=1))
            update = gate_t[:, i * n : (i + 2) * n] * update
            for d in range(2):
                z = z_t[i + d] + update[:, d * n : (d + 1) * n]
                if u == 0:
                    z_t[i + d] = z.astype(BF16).astype(F32)
                else:
                    out_ref[i + d] = jnp.transpose(z).astype(BF16)

    for u in range(2):
        for kind in ("near", "x"):
            all_blocks(u, kind).wait_send()
    all_blocks(0, "far").wait_send()


def fused_call(count, pair, residue_mask, *params):
    rows, n, chans = pair.shape
    hidden = params[-1].shape[1]
    per = rows * hidden // count
    args = (pair, residue_mask.reshape(1, n)) + params
    return pl.pallas_call(
        functools.partial(fused, count),
        out_shape=jax.ShapeDtypeStruct(pair.shape, BF16),
        in_specs=[pl.BlockSpec(memory_space=pltpu.HBM)] * len(args),
        out_specs=pl.BlockSpec(memory_space=pltpu.VMEM),
        scratch_shapes=[pltpu.VMEM(a.shape, a.dtype) for a in args]
        + [
            pltpu.SemaphoreType.DMA((len(args),)),
            pltpu.VMEM((rows, chans, n), F32),
            pltpu.VMEM((chans, rows * n), BF16),
            pltpu.VMEM((chans, rows * n), F32),
            pltpu.VMEM((hidden * 2 * rows, n), F32),
            pltpu.VMEM((4 * hidden, chans), BF16),
            pltpu.VMEM((count // 2, 2, 2 * per, n), BF16),
            pltpu.VMEM((count, 2, per, n), BF16),
            pltpu.VMEM((count, 2, 2 * per, n), BF16),
            pltpu.VMEM((count, 2, per, n), BF16),
            pltpu.VMEM((count // 2, 2 * per, n), BF16),
            pltpu.VMEM((count, per, n), BF16),
            pltpu.VMEM((count // 2, 2 * per, n), BF16),
            pltpu.VMEM((count, per, n), BF16),
            pltpu.VMEM((hidden * rows, n), F32),
            pltpu.SemaphoreType.DMA((2,)),
            pltpu.SemaphoreType.DMA((2,)),
            pltpu.SemaphoreType.DMA,
            pltpu.SemaphoreType.DMA,
            pltpu.SemaphoreType.DMA((2,)),
            pltpu.SemaphoreType.DMA((2,)),
        ],
        compiler_params=pltpu.CompilerParams(
            collective_id=0, has_side_effects=True, vmem_limit_bytes=63 * 1024 * 1024
        ),
        cost_estimate=pl.CostEstimate(
            flops=4 * rows * n * chans * (5 * hidden + n + hidden),
            bytes_accessed=4 * rows * n * chans,
            transcendentals=6 * rows * n * hidden,
        ),
    )(*args)


def per_device(count, fits, pair, *rest):
    rows, cols, chans = pair.shape
    hidden = rest[-1].shape[1]
    if (
        fits
        and rows == TILE
        and cols == rows * count == LANES
        and chans == LANES
        and hidden == LANES
        and hidden % (2 * count) == 0
        and count % 2 == 0
    ):
        return fused_call(count, pair, *rest)
    return shards(pair, *rest)


def solution(mesh):
    in_specs = (P(("group", "row"), "col", None), P("group"), P(), P(), P(), P(), P(), P(), P())
    out_specs = P(("group", "row"), "col", None)
    body = functools.partial(per_device, mesh.shape["row"], mesh.shape["col"] == 1)
    return jax.shard_map(body, mesh=mesh, in_specs=in_specs, out_specs=out_specs, check_vma=False)
```

```python
import functools

import jax
import jax.numpy as jnp
from jax import lax
from jax.experimental import pallas as pl
from jax.experimental.pallas import tpu as pltpu
from jax.sharding import PartitionSpec as P


def from_root(value, axis, source):
    kept = jnp.where(lax.axis_index(axis) == source, value, 0).astype(value.dtype)
    return lax.psum(kept, axis)


def layer_norm(v, gain, bias):
    mean = jnp.mean(v, axis=-1, keepdims=True)
    centred = v - mean
    var = jnp.mean(centred * centred, axis=-1, keepdims=True)
    return centred * lax.rsqrt(var + 1e-05) * gain + bias


def project(z, pm, layer, ln_gain, ln_bias, w_ab, w_gate):
    rows, cols, chans = z.shape
    hidden = w_ab.shape[2] // 4
    zn = layer_norm(z.astype(jnp.float32), ln_gain[layer], ln_bias[layer]).astype(jnp.bfloat16)
    flat = zn.reshape(rows * cols, chans)
    proj = jnp.dot(flat, w_ab[layer], preferred_element_type=jnp.float32).reshape(
        rows, cols, 4 * hidden
    )
    mask3 = pm[:, :, None]
    left = (jax.nn.sigmoid(proj[..., :hidden]) * proj[..., hidden : 2 * hidden] * mask3).astype(
        jnp.bfloat16
    )
    right = (
        jax.nn.sigmoid(proj[..., 2 * hidden : 3 * hidden]) * proj[..., 3 * hidden :] * mask3
    ).astype(jnp.bfloat16)
    gate = jax.nn.sigmoid(jnp.dot(flat, w_gate[layer], preferred_element_type=jnp.float32)).reshape(
        rows, cols, chans
    )
    return (left, right, gate)


def finish(z, x, gate, layer, out_gain, out_bias, w_out):
    rows, cols, chans = z.shape
    hidden = x.shape[2]
    xn = layer_norm(x, out_gain[layer], out_bias[layer]).astype(jnp.bfloat16)
    delta = jnp.dot(
        xn.reshape(rows * cols, hidden), w_out[layer], preferred_element_type=jnp.float32
    )
    return (z.astype(jnp.float32) + gate * delta.reshape(rows, cols, chans)).astype(jnp.bfloat16)


def shards(pair, residue_mask, ln_gain, ln_bias, w_ab, w_gate, out_gain, out_bias, w_out):
    rows, cols, chans = pair.shape
    hidden = w_out.shape[1]
    row_count = lax.axis_size("row")
    total = rows * row_count
    row_pos = lax.axis_index("row")
    col_pos = lax.axis_index("col")
    maskf = residue_mask.astype(jnp.float32)
    mask_rows = lax.dynamic_slice_in_dim(maskf, row_pos * rows, rows)
    mask_cols = lax.dynamic_slice_in_dim(maskf, col_pos * cols, cols)
    pm = mask_rows[:, None] * mask_cols[None, :]
    left, right, gate = project(pair, pm, 0, ln_gain, ln_bias, w_ab, w_gate)
    left_flat = left.reshape(rows, cols * hidden)
    right_flat = right.reshape(rows, cols * hidden)
    left_wide, right_wide = (
        lax.all_gather(left_flat, "col", axis=1, tiled=True),
        lax.all_gather(right_flat, "col", axis=1, tiled=True),
    )
    left_full = left_wide.reshape(rows, total, hidden)
    piece = lax.all_gather(right_wide, "row", axis=0, tiled=True)
    count = piece.shape[0]
    contrib = jnp.einsum(
        "ikc,jkc->ijc",
        left_full,
        piece.reshape(count, total, hidden),
        preferred_element_type=jnp.float32,
    )
    outgoing = lax.dynamic_slice_in_dim(contrib, col_pos * cols, cols, 1)
    first = finish(pair, outgoing, gate, 0, out_gain, out_bias, w_out)
    left, right, gate = project(first, pm, 1, ln_gain, ln_bias, w_ab, w_gate)
    blocks_half = cols // rows
    left_blocks = left.reshape(rows, blocks_half, rows * hidden)
    padded = jnp.zeros((rows, row_count, rows * hidden), jnp.bfloat16)
    padded = lax.dynamic_update_slice_in_dim(padded, left_blocks, col_pos * blocks_half, 1)
    received = lax.all_to_all(padded, "row", split_axis=1, concat_axis=0, tiled=True)
    owner = row_pos * rows // cols
    left_cols = from_root(received, "col", owner).reshape(total, rows, hidden)
    piece = lax.all_gather(right.reshape(rows, cols * hidden), "row", axis=0, tiled=True)
    count = piece.shape[0]
    incoming = jnp.einsum(
        "kic,kjc->ijc",
        left_cols,
        piece.reshape(count, cols, hidden),
        preferred_element_type=jnp.float32,
    )
    return finish(first, incoming, gate, 1, out_gain, out_bias, w_out)


F32 = jnp.float32
BF16 = jnp.bfloat16
TILE = 8
LANES = 128


def sigmoid(v):
    return 0.5 * jnp.tanh(0.5 * v) + 0.5


def matmul(a, b, contract=((1,), (0,))):
    return lax.dot_general(a, b, (contract, ((), ())), preferred_element_type=F32)


def column(ref, layer):
    row = ref[layer : layer + 1, :]
    return jnp.transpose(jnp.broadcast_to(row, (row.shape[1], row.shape[1])))


def fused(
    count,
    pair_hbm,
    mask_hbm,
    ln_gain_hbm,
    ln_bias_hbm,
    w_ab_hbm,
    w_gate_hbm,
    out_gain_hbm,
    out_bias_hbm,
    w_out_hbm,
    out_ref,
    pair_ref,
    mask_ref,
    ln_gain,
    ln_bias,
    w_ab,
    w_gate,
    out_gain,
    out_bias,
    w_out,
    load_sem,
    z_t,
    zn_t,
    gate_t,
    stage,
    w_next,
    edges0,
    edges1,
    in0,
    in1,
    x_out0,
    x_out1,
    x_in0,
    x_in1,
    x_wide,
    near_send,
    near_recv,
    far_send,
    far_recv,
    x_send,
    x_recv,
):
    rows, n, chans = pair_ref.shape
    hidden = w_out.shape[1]
    edges, edges_in = (edges0, edges1), (in0, in1)
    x_out, x_in = (x_out0, x_out1), (x_in0, x_in1)
    me = lax.axis_index("row")

    held = (pair_ref, mask_ref, ln_gain, ln_bias, w_ab, w_gate, out_gain, out_bias, w_out)
    given = (
        pair_hbm,
        mask_hbm,
        ln_gain_hbm,
        ln_bias_hbm,
        w_ab_hbm,
        w_gate_hbm,
        out_gain_hbm,
        out_bias_hbm,
        w_out_hbm,
    )
    loads = [
        pltpu.make_async_copy(src, dst, load_sem.at[k])
        for k, (src, dst) in enumerate(zip(given, held))
    ]
    for load in loads:
        load.start()

    barrier = pltpu.get_barrier_semaphore()

    def greet(step, carry):
        other = lax.rem(me + step, count)
        pl.semaphore_signal(
            barrier, inc=1, device_id={"row": other}, device_id_type=pl.DeviceIdType.MESH
        )
        return carry

    lax.fori_loop(1, count, greet, 0, unroll=True)

    def send(src, dst, send_sem, recv_sem, other):
        return pltpu.make_async_remote_copy(
            src_ref=src,
            dst_ref=dst,
            send_sem=send_sem,
            recv_sem=recv_sem,
            device_id={"row": other},
            device_id_type=pl.DeviceIdType.MESH,
        )

    def all_blocks(u, kind):
        if kind == "x":
            blocks = x_in[u].at[pl.ds(0, x_in[u].shape[0] - 1)]
            return send(blocks, blocks, x_send.at[u], x_recv.at[u], me)
        if kind == "near":
            blocks = edges_in[u].at[pl.ds(0, edges[u].shape[0] - 1)]
            return send(blocks, blocks, near_send.at[u], near_recv.at[u], me)
        blocks = edges_in[u].at[pl.ds(0, count - edges[u].shape[0]), 1]
        return send(blocks, blocks, far_send, far_recv, me)

    for load in loads[:5]:
        load.wait()
    mask_k = mask_ref[...].astype(F32)
    lane = lax.broadcasted_iota(jnp.int32, mask_k.shape, 1)
    masks = []
    for i in range(rows):
        mine = jnp.sum(jnp.where(lane == me * rows + i, mask_k, 0.0), axis=1, keepdims=True)
        masks.append(mask_k * mine)
    pm = [jnp.concatenate(masks[i : i + 2], axis=1) for i in range(0, rows, 2)]

    for u in range(2):
        team = count // 2 if u == 0 else count
        own = hidden // team
        size = own * rows
        member = lax.rem(me, team)
        base = me - member
        if u == 0:
            w_t = jnp.transpose(w_ab[u].astype(F32)).astype(BF16)
        else:
            w_t = w_next[...]
        gain, bias = column(ln_gain, u), column(ln_bias, u)
        for i in range(rows):
            if u == 0:
                z_t[i] = jnp.transpose(pair_ref[i].astype(F32))
            z = z_t[i]
            mean = jnp.mean(z, axis=0, keepdims=True)
            centred = z - mean
            var = jnp.mean(centred * centred, axis=0, keepdims=True)
            zn = centred * lax.rsqrt(var + 1e-05) * gain + bias
            zn_t[:, i * n : (i + 1) * n] = zn.astype(BF16)

        for i in range(0, rows, 2):
            proj = matmul(w_t, zn_t[:, i * n : (i + 2) * n])
            left = sigmoid(proj[:hidden]) * proj[hidden : 2 * hidden] * pm[i // 2]
            right = sigmoid(proj[2 * hidden : 3 * hidden]) * proj[3 * hidden :] * pm[i // 2]
            for d in range(2):
                at = slice(d * n, (d + 1) * n)
                stage[pl.ds(i + d, hidden, stride=rows), :] = left[:, at]
                stage[pl.ds(hidden * rows + i + d, hidden, stride=rows), :] = right[:, at]
        half = hidden * rows
        edges[u][:, 0] = stage[:half, :].astype(BF16).reshape(team, size, n)
        edges[u][:, 1] = stage[half:, :].astype(BF16).reshape(team, size, n)

        if u == 0:
            pl.semaphore_wait(barrier, count - 1)

        for step in range(1, team):
            to = lax.rem(member + step, team)
            near = edges_in[u].at[me]
            send(edges[u].at[to], near, near_send.at[u], near_recv.at[u], base + to).start()
            if team < count:
                to = lax.rem(member + step, team)
                far = edges_in[u].at[me, 1]
                other = lax.rem(base + team + to, count)
                send(edges[u].at[to, 1], far, far_send, far_recv, other).start()
        if team < count:
            far = edges_in[u].at[me, 1]
            other = lax.rem(me + team, count)
            send(edges[u].at[member, 1], far, far_send, far_recv, other).start()
        edges_in[u][me] = edges[u][member]

        if u == 0:
            for load in loads[5:]:
                load.wait()
        w_gate_t = jnp.transpose(w_gate[u].astype(F32)).astype(BF16)
        for i in range(0, rows, 2):
            at = slice(i * n, (i + 2) * n)
            gate_t[:, at] = sigmoid(matmul(w_gate_t, zn_t[:, at]))
        w_out_t = jnp.transpose(w_out[u].astype(F32)).astype(BF16)
        gain, bias = column(out_gain, u), column(out_bias, u)
        if u == 0:
            w_next[...] = jnp.transpose(w_ab[1].astype(F32)).astype(BF16)

        all_blocks(u, "near").wait_recv()
        if team < count:
            all_blocks(u, "far").wait_recv()
        for c in range(0, own, 2):
            at = slice(c * rows, (c + 2) * rows)
            lefts = edges_in[u][pl.ds(base, team), 0, at, :].astype(F32)
            rights = edges_in[u][:, 1, at, :].astype(F32)
            found = []
            for d in range(2):
                at_d = slice(d * rows, (d + 1) * rows)
                left = lefts[:, at_d].reshape(team * rows, n).astype(BF16)
                right = rights[:, at_d].reshape(n, n).astype(BF16)
                contract = ((1,), (1,)) if u == 0 else ((0,), (0,))
                found.append(matmul(left, right, contract).reshape(team, rows, n))
            x_out[u][:, at, :] = jnp.concatenate(found, axis=1).astype(BF16)

        for step in range(1, team):
            to = lax.rem(member + step, team)
            send(
                x_out[u].at[to], x_in[u].at[member], x_send.at[u], x_recv.at[u], base + to
            ).start()
        x_in[u][member] = x_out[u][member]
        all_blocks(u, "x").wait_recv()

        x = x_in[u][...].astype(F32).reshape(hidden, rows, n)
        mean = jnp.mean(x, axis=0)
        centred = x - mean[None]
        var = jnp.mean(centred * centred, axis=0)
        x_wide[...] = (centred * lax.rsqrt(var + 1e-05)[None]).reshape(hidden * rows, n)
        for i in range(0, rows, 2):
            xn = [
                (x_wide[pl.ds(i + d, hidden, stride=rows), :] * gain + bias).astype(BF16)
                for d in range(2)
            ]
            update = matmul(w_out_t, jnp.concatenate(xn, axis=1))
            update = gate_t[:, i * n : (i + 2) * n] * update
            for d in range(2):
                z = z_t[i + d] + update[:, d * n : (d + 1) * n]
                if u == 0:
                    z_t[i + d] = z.astype(BF16).astype(F32)
                else:
                    out_ref[i + d] = jnp.transpose(z).astype(BF16)

    for u in range(2):
        for kind in ("near", "x"):
            all_blocks(u, kind).wait_send()
    all_blocks(0, "far").wait_send()


def fused_call(count, pair, residue_mask, *params):
    rows, n, chans = pair.shape
    hidden = params[-1].shape[1]
    per = rows * hidden // count
    args = (pair, residue_mask.reshape(1, n)) + params
    return pl.pallas_call(
        functools.partial(fused, count),
        out_shape=jax.ShapeDtypeStruct(pair.shape, BF16),
        in_specs=[pl.BlockSpec(memory_space=pltpu.HBM)] * len(args),
        out_specs=pl.BlockSpec(memory_space=pltpu.VMEM),
        scratch_shapes=[pltpu.VMEM(a.shape, a.dtype) for a in args]
        + [
            pltpu.SemaphoreType.DMA((len(args),)),
            pltpu.VMEM((rows, chans, n), F32),
            pltpu.VMEM((chans, rows * n), BF16),
            pltpu.VMEM((chans, rows * n), F32),
            pltpu.VMEM((hidden * 2 * rows, n), F32),
            pltpu.VMEM((4 * hidden, chans), BF16),
            pltpu.VMEM((count // 2, 2, 2 * per, n), BF16),
            pltpu.VMEM((count, 2, per, n), BF16),
            pltpu.VMEM((count, 2, 2 * per, n), BF16),
            pltpu.VMEM((count, 2, per, n), BF16),
            pltpu.VMEM((count // 2, 2 * per, n), BF16),
            pltpu.VMEM((count, per, n), BF16),
            pltpu.VMEM((count // 2, 2 * per, n), BF16),
            pltpu.VMEM((count, per, n), BF16),
            pltpu.VMEM((hidden * rows, n), F32),
            pltpu.SemaphoreType.DMA((2,)),
            pltpu.SemaphoreType.DMA((2,)),
            pltpu.SemaphoreType.DMA,
            pltpu.SemaphoreType.DMA,
            pltpu.SemaphoreType.DMA((2,)),
            pltpu.SemaphoreType.DMA((2,)),
        ],
        compiler_params=pltpu.CompilerParams(
            collective_id=0, has_side_effects=True, vmem_limit_bytes=63 * 1024 * 1024
        ),
        cost_estimate=pl.CostEstimate(
            flops=4 * rows * n * chans * (5 * hidden + n + hidden),
            bytes_accessed=4 * rows * n * chans,
            transcendentals=6 * rows * n * hidden,
        ),
    )(*args)


def per_device(count, fits, pair, *rest):
    rows, cols, chans = pair.shape
    hidden = rest[-1].shape[1]
    if (
        fits
        and rows == TILE
        and cols == rows * count == LANES
        and chans == LANES
        and hidden == LANES
        and hidden % (2 * count) == 0
        and count % 2 == 0
    ):
        return fused_call(count, pair, *rest)
    return shards(pair, *rest)


def solution(mesh):
    in_specs = (P(("group", "row"), "col", None), P("group"), P(), P(), P(), P(), P(), P(), P())
    out_specs = P(("group", "row"), "col", None)
    body = functools.partial(per_device, mesh.shape["row"], mesh.shape["col"] == 1)
    return jax.shard_map(body, mesh=mesh, in_specs=in_specs, out_specs=out_specs, check_vma=False)
```
